32 devices in a mesh: energy: 8 (over y, x, core), dom: 4 (over z).
Axes of the slice: x: 2, y: 2, z: 4, core: 2. Of those that a mesh axis runs over, the one named last changes fastest.
Arguments:
- lesser_occupancy: float32 [8, 8, 128], P('energy', 'dom'), may hold values from 0.05 to 0.5
- greater_occupancy: float32 [8, 8, 128], P('energy', 'dom'), may hold values from 0.05 to 0.5
- hamiltonian: float32 [8, 2, 128, 128], P('dom'), as said below
- couplings: float32 [8, 2, 128, 128], P('dom')
- right_lead: float32 [2, 128, 128], replicated
- phonon_steps: int32 [6], replicated, may hold values from 1 to 4, as said below
- emission_strength: float32 [6], replicated, may hold values from 0.02 to 0.08
- absorption_strength: float32 [6], replicated, may hold values from 0.01 to 0.05
Outputs:
- green_diag: float32 [8, 8, 2, 128, 128], P('energy', 'dom')
- scattering_in: float32 [8, 8, 128], P('energy', 'dom')
- scattering_out: float32 [8, 8, 128], P('energy', 'dom')
The draws below stay inside these ranges and needn't reach their ends.
Inputs may be any that keep to these rules, and one draw needn't show every extreme that they name: `phonon_steps`: each mode's step in energy indices; some mode's step is 4. `hamiltonian`: every block is Hermitian: its real plane is symmetric and its imaginary plane antisymmetric.
All inputs are finite; a program needn't handle non-finite values.
Results may differ from the reference program's by a relative error of at most 0.00026.
Values sent between devices are 32-bit elements; how exact they have to be, the bound alone decides.
A program may use at most 64 MiB of HBM per device.

```python
import math
import jax
import jax.numpy as jnp
from jax import lax

ORB = 128
MODES = 6
SMAX = 4
NE = 8
NB = 8


def unit_planes(key, shape):
    return jax.random.normal(key, shape, jnp.float32)


def wire_planes(key, count):
    repeated = unit_planes(jax.random.fold_in(key, 1), (2, ORB, ORB))
    varying = unit_planes(jax.random.fold_in(key, 2), (count, 2, ORB, ORB))
    return repeated[None] + 0.05 * varying


def draw_hamiltonian(key, part):
    planes = wire_planes(jax.random.fold_in(key, 11), NB)
    real_part = 0.5 * (planes[:, 0] + jnp.swapaxes(planes[:, 0], -1, -2))
    imag_part = 0.5 * (planes[:, 1] - jnp.swapaxes(planes[:, 1], -1, -2))
    spread = 0.5 / ORB ** 0.5
    return (jnp.stack([real_part, imag_part], axis=1) * spread).astype(jnp.float32)


def draw_couplings(key, part):
    planes = wire_planes(jax.random.fold_in(key, 12), NB)
    spread = 0.6 / (2 * ORB) ** 0.5
    return (planes * spread).astype(jnp.float32)


def draw_right_lead(key, part):
    planes = unit_planes(jax.random.fold_in(key, 13), (2, ORB, ORB))
    spread = 0.6 / (2 * ORB) ** 0.5
    return (planes * spread).astype(jnp.float32)


def draw_phonon_steps(key, part):
    base_key = jax.random.fold_in(key, 14)
    first_key, second_key = jax.random.split(base_key)
    others = jax.random.randint(first_key, (MODES - 1,), 1, SMAX + 1)
    step_sizes = jnp.concatenate([jnp.full((1,), SMAX, jnp.int32), others.astype(jnp.int32)])
    arrangement = jax.random.permutation(second_key, MODES)
    return step_sizes[arrangement].astype(jnp.int32)


def block_scale(rng, extent, pieces, low, high):
    def one(axis_at, blocks):
        heights = jax.random.uniform(jax.random.fold_in(jax.random.fold_in(rng, 6), axis_at), (blocks,), jnp.float32, low / len(pieces), high / len(pieces))
        return jnp.repeat(jnp.exp(heights), extent[axis_at] // blocks).reshape((-1,) + (1,) * (len(extent) - axis_at - 1))

    factor_of = one(*pieces[0])
    for cut in pieces[1:]:
        factor_of = factor_of * one(*cut)
    return factor_of


def setup_inputs(seed: int = 0) -> dict:
    streams_of = jax.random.split(jax.random.key(seed), 9)
    lesser_occupancy = jnp.clip(jnp.exp(math.log(0.5) - 2.3025851 * jax.random.uniform(streams_of[0], (NE, NB, ORB), jnp.float32) ** block_scale(streams_of[0], (NE, NB, ORB), ((0, 8), (1, 4)), -0.2, 0.2)), 0.05, 0.5)
    greater_occupancy = jnp.clip(jnp.exp(math.log(0.5) - 2.3025851 * jax.random.uniform(streams_of[1], (NE, NB, ORB), jnp.float32) ** block_scale(streams_of[1], (NE, NB, ORB), ((0, 8), (1, 4)), -0.2, 0.2)), 0.05, 0.5)
    hamiltonian = draw_hamiltonian(jax.random.fold_in(streams_of[8], 71), 0)
    couplings = draw_couplings(jax.random.fold_in(streams_of[8], 71), 0)
    right_lead = draw_right_lead(jax.random.fold_in(streams_of[8], 71), 0)
    phonon_steps = draw_phonon_steps(jax.random.fold_in(streams_of[8], 71), 0)
    emission_strength = jnp.clip(jnp.exp(jax.random.uniform(streams_of[6], (MODES,), jnp.float32, math.log(0.02), math.log(0.08))), 0.02, 0.08)
    absorption_strength = jnp.clip(jnp.exp(jax.random.uniform(streams_of[7], (MODES,), jnp.float32, math.log(0.01), math.log(0.05))), 0.01, 0.05)
    return dict(lesser_occupancy=lesser_occupancy, greater_occupancy=greater_occupancy, hamiltonian=hamiltonian, couplings=couplings, right_lead=right_lead, phonon_steps=phonon_steps, emission_strength=emission_strength, absorption_strength=absorption_strength)


energy_low = -1.0
energy_span = 2.0
damping = 0.02

def complex_product(left_factor, right_factor):
    highest = lax.Precision.HIGHEST
    left_real = left_factor[..., 0, :, :]
    left_imag = left_factor[..., 1, :, :]
    right_real = right_factor[..., 0, :, :]
    right_imag = right_factor[..., 1, :, :]
    real_part = jnp.matmul(left_real, right_real, precision=highest) - jnp.matmul(left_imag, right_imag, precision=highest)
    imag_part = jnp.matmul(left_real, right_imag, precision=highest) + jnp.matmul(left_imag, right_real, precision=highest)
    return jnp.stack([real_part, imag_part], axis=-3)

def adjoint(matrix):
    return jnp.stack([jnp.swapaxes(matrix[..., 0, :, :], -1, -2), -jnp.swapaxes(matrix[..., 1, :, :], -1, -2)], axis=-3)

def complex_identity(like_block):
    order_size = like_block.shape[-1]
    unit_matrix = jnp.eye(order_size, dtype=like_block.dtype)
    planes = jnp.stack([unit_matrix, jnp.zeros_like(unit_matrix)])
    return jnp.broadcast_to(planes, like_block.shape)

def times_half_i(matrix):
    return jnp.stack([-0.5 * matrix[..., 1, :, :], 0.5 * matrix[..., 0, :, :]], axis=-3)

def invert(matrix):
    highest = lax.Precision.HIGHEST
    order_size = matrix.shape[-1]
    real_part = matrix[..., 0, :, :]
    imag_part = matrix[..., 1, :, :]
    upper_half = jnp.concatenate([real_part, -imag_part], axis=-1)
    lower_half = jnp.concatenate([imag_part, real_part], axis=-1)
    embedded = jnp.concatenate([upper_half, lower_half], axis=-2)
    transposed = jnp.swapaxes(embedded, -1, -2)
    normal_matrix = jnp.matmul(transposed, embedded, precision=highest)
    factor = jnp.linalg.cholesky(normal_matrix)
    solved = jax.scipy.linalg.cho_solve((factor, True), transposed[..., :order_size])
    estimate = jnp.stack([solved[..., :order_size, :], solved[..., order_size:, :]], axis=-3)
    residue = 2.0 * complex_identity(estimate) - complex_product(matrix, estimate)
    return complex_product(estimate, residue)

def reference(lesser_occupancy, greater_occupancy, hamiltonian, couplings, right_lead, phonon_steps, emission_strength, absorption_strength):
    energy_total = lesser_occupancy.shape[0]
    block_total = hamiltonian.shape[0]
    orbitals = hamiltonian.shape[-1]
    widths = ((SMAX, SMAX), (0, 0), (0, 0))
    lesser_padded = jnp.pad(lesser_occupancy, widths)
    greater_padded = jnp.pad(greater_occupancy, widths)
    scattering_in = jnp.zeros_like(lesser_occupancy)
    scattering_out = jnp.zeros_like(greater_occupancy)
    for mode_number in range(MODES):
        step_size = phonon_steps[mode_number]
        above_start = SMAX + step_size
        below_start = SMAX - step_size
        lesser_above = lax.dynamic_slice_in_dim(lesser_padded, above_start, energy_total, 0)
        lesser_below = lax.dynamic_slice_in_dim(lesser_padded, below_start, energy_total, 0)
        greater_above = lax.dynamic_slice_in_dim(greater_padded, above_start, energy_total, 0)
        greater_below = lax.dynamic_slice_in_dim(greater_padded, below_start, energy_total, 0)
        scattering_in = scattering_in + emission_strength[mode_number] * lesser_above + absorption_strength[mode_number] * lesser_below
        scattering_out = scattering_out + emission_strength[mode_number] * greater_below + absorption_strength[mode_number] * greater_above
    broadening = 0.5 * (scattering_in + scattering_out)
    positions = jnp.arange(energy_total, dtype=jnp.float32)
    energy_values = energy_low + energy_span * (positions + 0.5) / energy_total
    unit_matrix = jnp.eye(orbitals, dtype=jnp.float32)
    real_part = energy_values[:, None, None, None] * unit_matrix - hamiltonian[None, :, 0]
    imag_part = damping * unit_matrix - hamiltonian[None, :, 1] + unit_matrix * broadening[:, :, None, :]
    system = jnp.stack([real_part, imag_part], axis=2)
    first_lead = times_half_i(complex_product(adjoint(couplings[0]), couplings[0]))
    last_lead = times_half_i(complex_product(right_lead, adjoint(right_lead)))
    system = system.at[:, 0].add(first_lead)
    system = system.at[:, block_total - 1].add(last_lead)
    by_block = jnp.swapaxes(system, 0, 1)
    first_green = invert(by_block[0])

    def forward(previous, pair_items):
        block_matrix, link_block = pair_items
        coupled = complex_product(complex_product(adjoint(link_block), previous), link_block)
        current = invert(block_matrix - coupled)
        return (current, current)
    _, later_greens = lax.scan(forward, first_green, (by_block[1:], couplings[1:]))
    left_greens = jnp.concatenate([first_green[None], later_greens], axis=0)

    def backward(following, pair_items):
        own_green, link_block = pair_items
        carried = complex_product(complex_product(own_green, link_block), following)
        current = own_green + complex_product(complex_product(carried, adjoint(link_block)), own_green)
        return (current, current)
    last_green = left_greens[-1]
    _, earlier = lax.scan(backward, last_green, (left_greens[:-1], couplings[1:]), reverse=True)
    diagonal = jnp.concatenate([earlier, last_green[None]], axis=0)
    return (jnp.swapaxes(diagonal, 0, 1), scattering_in, scattering_out)
```

```python
import functools

import jax
import jax.numpy as jnp
from jax import lax
from jax.experimental import pallas as pl
from jax.experimental.pallas import tpu as pltpu
from jax.sharding import PartitionSpec as P

MODES = 6
SMAX = 4
N = 128
H = 64
B = 8

energy_low = -1.0
energy_span = 2.0
damping = 0.02

MESH = pl.DeviceIdType.MESH


def product(a, b):
    h = b.shape[1] // 2
    turned_rows = jnp.concatenate([-b[:, h:], b[:, :h]], axis=1)
    return jnp.dot(
        a,
        jnp.concatenate([b, turned_rows], axis=0),
        precision=lax.Precision.HIGHEST,
        preferred_element_type=jnp.float32,
    )


def adjoint(a):
    return jnp.concatenate([a[:, :N].T, -a[:, N:].T], axis=1)


def identity():
    row = lax.broadcasted_iota(jnp.int32, (N, 2 * N), 0)
    lane = lax.broadcasted_iota(jnp.int32, (N, 2 * N), 1)
    return jnp.where(row == lane, 1.0, 0.0)


def times_i(a):
    r = pltpu.roll(a, H, axis=1)
    return jnp.where(lax.broadcasted_iota(jnp.int32, a.shape, 1) < H, -r, r)


def invert_half(x):
    shape = (B, N)
    row = lax.broadcasted_iota(jnp.int32, shape, 0)
    lane = lax.broadcasted_iota(jnp.int32, shape, 1)
    column = lane % H
    groups = [x[i * B : (i + 1) * B] for i in range(H // B)]
    count = len(groups)

    def along_lanes(v, c):
        return jnp.broadcast_to(v[:, c : c + 1], shape)

    def along_rows(v, k):
        return jnp.broadcast_to(v[k : k + 1], shape)

    for p in range(count):
        panel = groups[p]
        turned = times_i(panel)
        br = [along_lanes(panel, p * B + j) for j in range(B)]
        bi = [along_lanes(panel, H + p * B + j) for j in range(B)]
        for k in range(B):
            own = row == k
            qr = along_rows(br[k], k)
            qi = along_rows(bi[k], k)
            s = 1.0 / (qr * qr + qi * qi)
            vr = qr * s
            vi = -qi * s
            mr = jnp.where(own, 0.0, br[k])
            mi = jnp.where(own, 0.0, bi[k])
            here = column == p * B + k
            panel = jnp.where(here, jnp.where(own & (lane < H), 1.0, 0.0), panel)
            turned = jnp.where(here, jnp.where(own & (lane >= H), 1.0, 0.0), turned)
            y = along_rows(panel, k)
            ty = along_rows(turned, k)
            r = y * vr + ty * vi
            tr = ty * vr - y * vi
            panel = jnp.where(own, r, panel - (mr * r + mi * tr))
            turned = jnp.where(own, tr, turned - (mr * tr - mi * r))
            for j in range(k + 1, B):
                yr = along_rows(br[j], k)
                yi = along_rows(bi[j], k)
                rr = yr * vr - yi * vi
                ri = yr * vi + yi * vr
                br[j] = jnp.where(own, rr, br[j] - (mr * rr - mi * ri))
                bi[j] = jnp.where(own, ri, bi[j] - (mr * ri + mi * rr))
        groups[p] = panel
        inside = (column >= p * B) & (column < (p + 1) * B)
        rr = [along_rows(panel, j) for j in range(B)]
        ri = [along_rows(turned, j) for j in range(B)]
        for t in range(1, count):
            g = (p + t) % count
            old = groups[g]
            new = jnp.where(inside, 0.0, old)
            for j in range(B):
                new = new - (
                    along_lanes(old, p * B + j) * rr[j] + along_lanes(old, H + p * B + j) * ri[j]
                )
            groups[g] = new
    return jnp.concatenate(groups, axis=0)


def quarter(x, i, j):
    rows = x[i * H : (i + 1) * H]
    return jnp.concatenate(
        [rows[:, j * H : (j + 1) * H], rows[:, N + j * H : N + (j + 1) * H]], axis=1
    )


def invert_into(x, out_ref):
    a, b, c, d = quarter(x, 0, 0), quarter(x, 0, 1), quarter(x, 1, 0), quarter(x, 1, 1)
    e = invert_half(a)
    f = product(e, b)
    g = product(c, e)
    s = invert_half(d - product(c, f))
    fs = product(f, s)
    first = e + product(fs, g)
    across = -fs
    back = -product(s, g)
    out_ref[:H] = jnp.concatenate(
        [first[:, :H], across[:, :H], first[:, H:], across[:, H:]], axis=1
    )
    out_ref[H:] = jnp.concatenate([back[:, :H], s[:, :H], back[:, H:], s[:, H:]], axis=1)


def kernel(
    energy_count,
    partitions,
    steps_ref,
    emission_ref,
    absorption_ref,
    lesser_ref,
    greater_ref,
    ham_ref,
    coupling_ref,
    lead_ref,
    green_ref,
    in_ref,
    out_ref,
    own_ref,
    window_ref,
    received,
    outgoing,
    a_first,
    a_second,
    c_fs,
    c_sf,
    w,
    wd,
    f_ref,
    u_ref,
    t_ref,
    s_ref,
    g_ref,
    th_ref,
    ht_ref,
    hb_ref,
    sig_ref,
    y_ref,
    uy_ref,
    q_ref,
    x_ref,
    r_ref,
    occ_send,
    occ_recv,
    dom_send,
    dom_recv,
):
    energy = lax.axis_index("energy")
    dom = lax.axis_index("dom")
    half = (2 * dom >= partitions).astype(jnp.int32)
    left_half = half == 0
    right_half = half == 1
    has_early = jnp.where(left_half, dom, partitions - 1 - dom) > 0
    offsets = [o for o in range(-SMAX, SMAX + 1) if o != 0]

    def in_range(o):
        return (energy + o >= 0) & (energy + o < energy_count)

    barrier = pltpu.get_barrier_semaphore()
    greeted = jnp.int32(0)
    for o in offsets:
        there = in_range(o)
        greeted = greeted + there.astype(jnp.int32)

        @pl.when(there)
        def _():
            pl.semaphore_signal(
                barrier, inc=1, device_id={"energy": energy + o}, device_id_type=MESH
            )

    for o in (-1, 1):
        there = (dom + o >= 0) & (dom + o < partitions)
        greeted = greeted + there.astype(jnp.int32)

        @pl.when(there)
        def _():
            pl.semaphore_signal(barrier, inc=1, device_id={"dom": dom + o}, device_id_type=MESH)

    own_ref[0:2] = lesser_ref[0]
    own_ref[2:4] = greater_ref[0]
    own_ref[4:8] = jnp.zeros((4, N), jnp.float32)
    pl.semaphore_wait(barrier, greeted)

    def occupancy_copy(number, o):
        return pltpu.make_async_remote_copy(
            src_ref=own_ref,
            dst_ref=window_ref.at[len(offsets) - 1 - number],
            send_sem=occ_send.at[number],
            recv_sem=occ_recv.at[len(offsets) - 1 - number],
            device_id={"energy": energy + o},
            device_id_type=MESH,
        )

    for number, o in enumerate(offsets):
        there = in_range(o)

        @pl.when(there)
        def _():
            occupancy_copy(number, o).start()

        @pl.when(jnp.logical_not(there))
        def _():
            window_ref[number] = jnp.zeros((8, N), jnp.float32)

    link = jnp.concatenate([coupling_ref[1, 0], coupling_ref[1, 1]], axis=1)
    link_adjoint = adjoint(link)
    outer = jnp.concatenate([coupling_ref[0, 0], coupling_ref[0, 1]], axis=1)
    outer_adjoint = adjoint(outer)
    w[...] = outer
    wd[...] = outer_adjoint

    @pl.when(left_half)
    def _():
        c_fs[...] = link
        c_sf[...] = link_adjoint

    @pl.when(right_half)
    def _():
        c_fs[...] = link_adjoint
        c_sf[...] = link

    @pl.when(has_early)
    def _():
        x_ref[...] = jnp.zeros((N, 2 * N), jnp.float32)

    def half_i(a):
        return jnp.concatenate([-0.5 * a[:, N:], 0.5 * a[:, :N]], axis=1)

    @pl.when(dom == 0)
    def _():
        x_ref[...] = half_i(product(wd[...], w[...]))

    @pl.when(dom == partitions - 1)
    def _():
        lead = jnp.concatenate([lead_ref[0], lead_ref[1]], axis=1)
        x_ref[...] = half_i(product(lead, adjoint(lead)))

    for number, o in enumerate(offsets):

        @pl.when(in_range(o))
        def _():
            occupancy_copy(len(offsets) - 1 - number, -o).wait_recv()

    scattering_in = jnp.zeros((2, N), jnp.float32)
    scattering_out = jnp.zeros((2, N), jnp.float32)
    for step in range(1, SMAX + 1):
        emission = jnp.float32(0.0)
        absorption = jnp.float32(0.0)
        for m in range(MODES):
            chosen = steps_ref[m] == step
            emission = emission + jnp.where(chosen, emission_ref[m], 0.0)
            absorption = absorption + jnp.where(chosen, absorption_ref[m], 0.0)
        above = window_ref[offsets.index(step)]
        below = window_ref[offsets.index(-step)]
        scattering_in = scattering_in + emission * above[0:2] + absorption * below[0:2]
        scattering_out = scattering_out + emission * below[2:4] + absorption * above[2:4]
    in_ref[0] = scattering_in
    out_ref[0] = scattering_out
    broadening = 0.5 * (scattering_in + scattering_out)

    position = jnp.full((N, N), energy, jnp.int32).astype(jnp.float32)
    energy_value = energy_low + energy_span * (position + 0.5) / energy_count
    unit = identity()[:, :N]

    def system(b):
        real_part = unit * energy_value - ham_ref[b, 0]
        imag_part = unit * (damping + broadening[b : b + 1]) - ham_ref[b, 1]
        return jnp.concatenate([real_part, imag_part], axis=1)

    block_0 = system(0)
    block_1 = system(1)

    @pl.when(left_half)
    def _():
        a_first[...] = block_0 + x_ref[...]
        a_second[...] = block_1

    @pl.when(right_half)
    def _():
        a_first[...] = block_1 + x_ref[...]
        a_second[...] = block_0

    def early_copy():
        return pltpu.make_async_remote_copy(
            src_ref=outgoing.at[0],
            dst_ref=received.at[half],
            send_sem=dom_send.at[0],
            recv_sem=dom_recv.at[half],
            device_id={"dom": dom + 1 - 2 * half},
            device_id_type=MESH,
        )

    def late_copy():
        return pltpu.make_async_remote_copy(
            src_ref=outgoing.at[1],
            dst_ref=received.at[1 - half],
            send_sem=dom_send.at[1],
            recv_sem=dom_recv.at[1 - half],
            device_id={"dom": dom - 1 + 2 * half},
            device_id_type=MESH,
        )

    def wrap_out(v):
        return product(product(w[...], v), wd[...])

    def wrap_in(v):
        return product(product(wd[...], v), w[...])

    def send_early(v):
        @pl.when(left_half)
        def _():
            outgoing[0] = v

        @pl.when(right_half)
        def _():
            outgoing[0] = wrap_out(v)

        early_copy().start()

    def stage(number, carry):
        @pl.when(has_early | ((number != 2) & (number != 4)))
        def _():
            @pl.when(number == 0)
            def _():
                x_ref[...] = a_first[...]

            @pl.when(number == 1)
            def _():
                x_ref[...] = s_ref[...]

            @pl.when(number == 2)
            def _():
                early_copy().wait_recv()

                @pl.when(left_half)
                def _():
                    sig_ref[...] = wrap_in(received[0])

                @pl.when(right_half)
                def _():
                    sig_ref[...] = received[1]

                x_ref[...] = identity() - product(hb_ref[...], sig_ref[...])

            @pl.when(number == 3)
            def _():
                late_copy().wait_recv()

                @pl.when(left_half)
                def _():
                    x_ref[...] = s_ref[...] - received[1]

                @pl.when(right_half)
                def _():
                    x_ref[...] = s_ref[...] - wrap_in(received[0])

            @pl.when(number == 4)
            def _():
                x_ref[...] = identity() - product(q_ref[...], sig_ref[...])

            invert_into(x_ref[...], r_ref)

            @pl.when(number == 0)
            def _():
                f = r_ref[...]
                t = product(c_sf[...], f)
                f_ref[...] = f
                t_ref[...] = t
                s_ref[...] = a_second[...] - product(t, c_fs[...])
                u_ref[...] = product(f, c_fs[...])

            @pl.when(number == 1)
            def _():
                g = r_ref[...]
                g_ref[...] = g

                @pl.when(jnp.logical_not(has_early))
                def _():
                    send_early(g)

                @pl.when(has_early)
                def _():
                    ht = product(u_ref[...], g)
                    ht_ref[...] = ht
                    hb_ref[...] = f_ref[...] + product(ht, t_ref[...])
                    th_ref[...] = product(g, t_ref[...])

            @pl.when(number == 2)
            def _():
                z = product(sig_ref[...], r_ref[...])
                send_early(g_ref[...] + product(product(th_ref[...], z), ht_ref[...]))

            @pl.when(number == 3)
            def _():
                y = r_ref[...]
                uy = product(u_ref[...], y)
                q = f_ref[...] + product(uy, t_ref[...])
                y_ref[...] = y
                uy_ref[...] = uy
                q_ref[...] = q

                @pl.when(has_early)
                def _():
                    @pl.when(left_half)
                    def _():
                        outgoing[1] = wrap_out(q)

                    @pl.when(right_half)
                    def _():
                        outgoing[1] = q

                    late_copy().start()

            @pl.when(number == 4)
            def _():
                m = r_ref[...]
                y = y_ref[...]
                z = product(sig_ref[...], m)
                yt = product(y, t_ref[...])
                y_ref[...] = y + product(product(yt, z), uy_ref[...])
                q_ref[...] = product(m, q_ref[...])

        return carry

    lax.fori_loop(0, 5, stage, 0)

    def put(block, v):
        green_ref[0, block, 0] = v[:, :N]
        green_ref[0, block, 1] = v[:, N:]

    @pl.when(left_half)
    def _():
        put(0, q_ref[...])
        put(1, y_ref[...])

    @pl.when(right_half)
    def _():
        put(0, y_ref[...])
        put(1, q_ref[...])

    for number, o in enumerate(offsets):

        @pl.when(in_range(o))
        def _():
            occupancy_copy(number, o).wait_send()

    early_copy().wait_send()

    @pl.when(has_early)
    def _():
        late_copy().wait_send()


def local(
    lesser_occupancy,
    greater_occupancy,
    hamiltonian,
    couplings,
    right_lead,
    phonon_steps,
    emission_strength,
    absorption_strength,
):
    whole = pl.BlockSpec(memory_space=pltpu.VMEM)
    scalars = pl.BlockSpec(memory_space=pltpu.SMEM)
    matrix = pltpu.VMEM((N, 2 * N), jnp.float32)
    pair = pltpu.VMEM((2, N, 2 * N), jnp.float32)
    reach = 2 * SMAX
    return pl.pallas_call(
        functools.partial(kernel, lax.axis_size("energy"), lax.axis_size("dom")),
        out_shape=(
            jax.ShapeDtypeStruct((1, 2, 2, N, N), jnp.float32),
            jax.ShapeDtypeStruct((1, 2, N), jnp.float32),
            jax.ShapeDtypeStruct((1, 2, N), jnp.float32),
        ),
        in_specs=[scalars] * 3 + [whole] * 5,
        out_specs=(whole,) * 3,
        scratch_shapes=[
            pltpu.VMEM((8, N), jnp.float32),
            pltpu.VMEM((reach, 8, N), jnp.float32),
            pair,
            pair,
        ]
        + [matrix] * 20
        + [
            pltpu.SemaphoreType.DMA((reach,)),
            pltpu.SemaphoreType.DMA((reach,)),
            pltpu.SemaphoreType.DMA((2,)),
            pltpu.SemaphoreType.DMA((2,)),
        ],
        compiler_params=pltpu.CompilerParams(
            collective_id=0, has_side_effects=True, vmem_limit_bytes=40 * 2**20
        ),
    )(
        phonon_steps,
        emission_strength,
        absorption_strength,
        lesser_occupancy,
        greater_occupancy,
        hamiltonian,
        couplings,
        right_lead,
    )


def solution(mesh):
    return jax.shard_map(
        local,
        mesh=mesh,
        in_specs=(
            P("energy", "dom", None),
            P("energy", "dom", None),
            P("dom", None, None, None),
            P("dom", None, None, None),
            P(),
            P(),
            P(),
            P(),
        ),
        out_specs=(
            P("energy", "dom", None, None, None),
            P("energy", "dom", None),
            P("energy", "dom", None),
        ),
        check_vma=False,
    )
```

```python
import functools

import jax
import jax.numpy as jnp
from jax import lax
from jax.experimental import pallas as pl
from jax.experimental.pallas import tpu as pltpu
from jax.sharding import PartitionSpec as P

MODES = 6
SMAX = 4
N = 128
H = 64
B = 8

energy_low = -1.0
energy_span = 2.0
damping = 0.02

MESH = pl.DeviceIdType.MESH


def parts(v):
    high = v.astype(jnp.bfloat16)
    return high, (v - high.astype(jnp.float32)).astype(jnp.bfloat16)


def real_product(a, b):
    a_high, a_low = parts(a)
    b_high, b_low = parts(b)
    dot = functools.partial(jnp.dot, preferred_element_type=jnp.float32)
    return dot(a_high, b_high) + (dot(a_high, b_low) + dot(a_low, b_high))


def product(a, b):
    h = b.shape[1] // 2
    turned_rows = jnp.concatenate([-b[:, h:], b[:, :h]], axis=1)
    return real_product(a, jnp.concatenate([b, turned_rows], axis=0))


def adjoint(a):
    return jnp.concatenate([a[:, :N].T, -a[:, N:].T], axis=1)


def identity():
    row = lax.broadcasted_iota(jnp.int32, (N, 2 * N), 0)
    lane = lax.broadcasted_iota(jnp.int32, (N, 2 * N), 1)
    return jnp.where(row == lane, 1.0, 0.0)


def times_i(a):
    r = pltpu.roll(a, H, axis=1)
    return jnp.where(lax.broadcasted_iota(jnp.int32, a.shape, 1) < H, -r, r)


def invert_half(x):
    shape = (B, N)
    row = lax.broadcasted_iota(jnp.int32, shape, 0)
    lane = lax.broadcasted_iota(jnp.int32, shape, 1)
    column = lane % H
    groups = [x[i * B : (i + 1) * B] for i in range(H // B)]
    count = len(groups)

    def along_lanes(v, c):
        return jnp.broadcast_to(v[:, c : c + 1], shape)

    def along_rows(v, k):
        return jnp.broadcast_to(v[k : k + 1], shape)

    zero = jnp.zeros(shape, jnp.float32)
    for p in range(count):
        panel = groups[p]
        turned = times_i(panel)
        br = [along_lanes(panel, p * B + j) for j in range(B)]
        bi = [along_lanes(panel, H + p * B + j) for j in range(B)]
        sr = zero
        si = zero
        for k in range(B):
            own = row == k
            mr = jnp.where(own, 0.0, br[k])
            mi = jnp.where(own, 0.0, bi[k])
            qr = along_rows(br[k], k)
            qi = along_rows(bi[k], k)
            s = 1.0 / (qr * qr + qi * qi)
            ur = (mr * qr + mi * qi) * s
            ui = (mi * qr - mr * qi) * s
            sr = jnp.where(own, qr * s, sr)
            si = jnp.where(own, -qi * s, si)
            for j in range(k + 1, B):
                yr = along_rows(br[j], k)
                yi = along_rows(bi[j], k)
                br[j] = br[j] - (ur * yr - ui * yi)
                bi[j] = bi[j] - (ur * yi + ui * yr)
            here = column == p * B + k
            panel = jnp.where(here, jnp.where(own & (lane < H), 1.0, 0.0), panel)
            turned = jnp.where(here, jnp.where(own & (lane >= H), 1.0, 0.0), turned)
            y = along_rows(panel, k)
            ty = along_rows(turned, k)
            panel = panel - (ur * y + ui * ty)
            turned = turned - (ur * ty - ui * y)
        panel, turned = sr * panel + si * turned, sr * turned - si * panel
        old = list(groups)
        groups[p] = panel
        inside = (column >= p * B) & (column < (p + 1) * B)
        spread = [zero] * p + [panel] + [zero] * (count - 1) + [turned] + [zero] * (count - 1 - p)
        change = real_product(jnp.concatenate(old, axis=0), jnp.concatenate(spread, axis=0))
        for g in range(count):
            if g == p:
                continue
            new = jnp.where(inside, 0.0, old[g])
            if g == p + 1:
                for j in range(B):
                    new = new - (
                        along_lanes(old[g], p * B + j) * along_rows(panel, j)
                        + along_lanes(old[g], H + p * B + j) * along_rows(turned, j)
                    )
            else:
                new = new - change[g * B : (g + 1) * B]
            groups[g] = new
    return jnp.concatenate(groups, axis=0)


def quarter(x, i, j):
    rows = x[i * H : (i + 1) * H]
    return jnp.concatenate(
        [rows[:, j * H : (j + 1) * H], rows[:, N + j * H : N + (j + 1) * H]], axis=1
    )


def invert_into(x, out_ref):
    a, b, c, d = quarter(x, 0, 0), quarter(x, 0, 1), quarter(x, 1, 0), quarter(x, 1, 1)
    e = invert_half(a)
    f = product(e, b)
    g = product(c, e)
    s = invert_half(d - product(c, f))
    fs = product(f, s)
    first = e + product(fs, g)
    across = -fs
    back = -product(s, g)
    out_ref[:H] = jnp.concatenate(
        [first[:, :H], across[:, :H], first[:, H:], across[:, H:]], axis=1
    )
    out_ref[H:] = jnp.concatenate([back[:, :H], s[:, :H], back[:, H:], s[:, H:]], axis=1)


def kernel(
    energy_count,
    partitions,
    steps_hbm,
    emission_hbm,
    absorption_hbm,
    lesser_hbm,
    greater_hbm,
    ham_hbm,
    coupling_hbm,
    lead_hbm,
    green_ref,
    in_ref,
    out_ref,
    steps_ref,
    emission_ref,
    absorption_ref,
    lesser_ref,
    greater_ref,
    ham_ref,
    coupling_ref,
    lead_ref,
    own_ref,
    window_ref,
    received,
    outgoing,
    a_first,
    a_second,
    c_fs,
    c_sf,
    w,
    wd,
    f_ref,
    u_ref,
    t_ref,
    s_ref,
    g_ref,
    th_ref,
    ht_ref,
    hb_ref,
    sig_ref,
    y_ref,
    uy_ref,
    q_ref,
    x_ref,
    r_ref,
    occ_send,
    occ_recv,
    dom_send,
    dom_recv,
    fetch_sems,
):
    fetches = [
        pltpu.make_async_copy(src, dst, fetch_sems.at[number])
        for number, (src, dst) in enumerate(
            (
                (lesser_hbm, lesser_ref),
                (greater_hbm, greater_ref),
                (coupling_hbm, coupling_ref),
                (lead_hbm, lead_ref),
                (steps_hbm, steps_ref),
                (emission_hbm, emission_ref),
                (absorption_hbm, absorption_ref),
                (ham_hbm, ham_ref),
            )
        )
    ]
    for fetch in fetches:
        fetch.start()
    energy = lax.axis_index("energy")
    dom = lax.axis_index("dom")
    half = (2 * dom >= partitions).astype(jnp.int32)
    left_half = half == 0
    right_half = half == 1
    has_early = jnp.where(left_half, dom, partitions - 1 - dom) > 0
    offsets = [o for o in range(-SMAX, SMAX + 1) if o != 0]

    def in_range(o):
        return (energy + o >= 0) & (energy + o < energy_count)

    barrier = pltpu.get_barrier_semaphore()
    greeted = jnp.int32(0)
    for o in offsets:
        there = in_range(o)
        greeted = greeted + there.astype(jnp.int32)

        @pl.when(there)
        def _():
            pl.semaphore_signal(
                barrier, inc=1, device_id={"energy": energy + o}, device_id_type=MESH
            )

    for o in (-1, 1):
        there = (dom + o >= 0) & (dom + o < partitions)
        greeted = greeted + there.astype(jnp.int32)

        @pl.when(there)
        def _():
            pl.semaphore_signal(barrier, inc=1, device_id={"dom": dom + o}, device_id_type=MESH)

    fetches[0].wait()
    fetches[1].wait()
    own_ref[0:2] = lesser_ref[0]
    own_ref[2:4] = greater_ref[0]
    own_ref[4:8] = jnp.zeros((4, N), jnp.float32)
    pl.semaphore_wait(barrier, greeted)

    def occupancy_copy(number, o):
        return pltpu.make_async_remote_copy(
            src_ref=own_ref,
            dst_ref=window_ref.at[len(offsets) - 1 - number],
            send_sem=occ_send.at[number],
            recv_sem=occ_recv.at[len(offsets) - 1 - number],
            device_id={"energy": energy + o},
            device_id_type=MESH,
        )

    for number, o in enumerate(offsets):
        there = in_range(o)

        @pl.when(there)
        def _():
            occupancy_copy(number, o).start()

        @pl.when(jnp.logical_not(there))
        def _():
            window_ref[number] = jnp.zeros((8, N), jnp.float32)

    for fetch in fetches[2:]:
        fetch.wait()
    link = jnp.concatenate([coupling_ref[1, 0], coupling_ref[1, 1]], axis=1)
    link_adjoint = adjoint(link)
    outer = jnp.concatenate([coupling_ref[0, 0], coupling_ref[0, 1]], axis=1)
    outer_adjoint = adjoint(outer)
    w[...] = outer
    wd[...] = outer_adjoint

    @pl.when(left_half)
    def _():
        c_fs[...] = link
        c_sf[...] = link_adjoint

    @pl.when(right_half)
    def _():
        c_fs[...] = link_adjoint
        c_sf[...] = link

    @pl.when(has_early)
    def _():
        x_ref[...] = jnp.zeros((N, 2 * N), jnp.float32)

    def half_i(a):
        return jnp.concatenate([-0.5 * a[:, N:], 0.5 * a[:, :N]], axis=1)

    @pl.when(dom == 0)
    def _():
        x_ref[...] = half_i(product(wd[...], w[...]))

    @pl.when(dom == partitions - 1)
    def _():
        lead = jnp.concatenate([lead_ref[0], lead_ref[1]], axis=1)
        x_ref[...] = half_i(product(lead, adjoint(lead)))

    for number, o in enumerate(offsets):

        @pl.when(in_range(o))
        def _():
            occupancy_copy(len(offsets) - 1 - number, -o).wait_recv()

    scattering_in = jnp.zeros((2, N), jnp.float32)
    scattering_out = jnp.zeros((2, N), jnp.float32)
    for step in range(1, SMAX + 1):
        emission = jnp.float32(0.0)
        absorption = jnp.float32(0.0)
        for m in range(MODES):
            chosen = steps_ref[m] == step
            emission = emission + jnp.where(chosen, emission_ref[m], 0.0)
            absorption = absorption + jnp.where(chosen, absorption_ref[m], 0.0)
        above = window_ref[offsets.index(step)]
        below = window_ref[offsets.index(-step)]
        scattering_in = scattering_in + emission * above[0:2] + absorption * below[0:2]
        scattering_out = scattering_out + emission * below[2:4] + absorption * above[2:4]
    in_ref[0] = scattering_in
    out_ref[0] = scattering_out
    broadening = 0.5 * (scattering_in + scattering_out)

    position = jnp.full((N, N), energy, jnp.int32).astype(jnp.float32)
    energy_value = energy_low + energy_span * (position + 0.5) / energy_count
    unit = identity()[:, :N]

    def system(b):
        real_part = unit * energy_value - ham_ref[b, 0]
        imag_part = unit * (damping + broadening[b : b + 1]) - ham_ref[b, 1]
        return jnp.concatenate([real_part, imag_part], axis=1)

    block_0 = system(0)
    block_1 = system(1)

    @pl.when(left_half)
    def _():
        a_first[...] = block_0 + x_ref[...]
        a_second[...] = block_1

    @pl.when(right_half)
    def _():
        a_first[...] = block_1 + x_ref[...]
        a_second[...] = block_0

    def early_copy():
        return pltpu.make_async_remote_copy(
            src_ref=outgoing.at[0],
            dst_ref=received.at[half],
            send_sem=dom_send.at[0],
            recv_sem=dom_recv.at[half],
            device_id={"dom": dom + 1 - 2 * half},
            device_id_type=MESH,
        )

    def late_copy():
        return pltpu.make_async_remote_copy(
            src_ref=outgoing.at[1],
            dst_ref=received.at[1 - half],
            send_sem=dom_send.at[1],
            recv_sem=dom_recv.at[1 - half],
            device_id={"dom": dom - 1 + 2 * half},
            device_id_type=MESH,
        )

    def wrap_out(v):
        return product(product(w[...], v), wd[...])

    def wrap_in(v):
        return product(product(wd[...], v), w[...])

    def send_early(v):
        @pl.when(left_half)
        def _():
            outgoing[0] = v

        @pl.when(right_half)
        def _():
            outgoing[0] = wrap_out(v)

        early_copy().start()

    def stage(number, carry):
        @pl.when(has_early | ((number != 2) & (number != 4)))
        def _():
            @pl.when(number == 0)
            def _():
                x_ref[...] = a_first[...]

            @pl.when(number == 1)
            def _():
                x_ref[...] = s_ref[...]

            @pl.when(number == 2)
            def _():
                early_copy().wait_recv()

                @pl.when(left_half)
                def _():
                    sig_ref[...] = wrap_in(received[0])

                @pl.when(right_half)
                def _():
                    sig_ref[...] = received[1]

                x_ref[...] = identity() - product(hb_ref[...], sig_ref[...])

            @pl.when(number == 3)
            def _():
                late_copy().wait_recv()

                @pl.when(left_half)
                def _():
                    x_ref[...] = s_ref[...] - received[1]

                @pl.when(right_half)
                def _():
                    x_ref[...] = s_ref[...] - wrap_in(received[0])

            @pl.when(number == 4)
            def _():
                x_ref[...] = identity() - product(q_ref[...], sig_ref[...])

            invert_into(x_ref[...], r_ref)

            @pl.when(number == 0)
            def _():
                f = r_ref[...]
                t = product(c_sf[...], f)
                f_ref[...] = f
                t_ref[...] = t
                s_ref[...] = a_second[...] - product(t, c_fs[...])
                u_ref[...] = product(f, c_fs[...])

            @pl.when(number == 1)
            def _():
                g = r_ref[...]
                g_ref[...] = g

                @pl.when(jnp.logical_not(has_early))
                def _():
                    send_early(g)

                @pl.when(has_early)
                def _():
                    ht = product(u_ref[...], g)
                    ht_ref[...] = ht
                    hb_ref[...] = f_ref[...] + product(ht, t_ref[...])
                    th_ref[...] = product(g, t_ref[...])

            @pl.when(number == 2)
            def _():
                z = product(sig_ref[...], r_ref[...])
                send_early(g_ref[...] + product(product(th_ref[...], z), ht_ref[...]))

            @pl.when(number == 3)
            def _():
                y = r_ref[...]
                uy = product(u_ref[...], y)
                q = f_ref[...] + product(uy, t_ref[...])
                y_ref[...] = y
                uy_ref[...] = uy
                q_ref[...] = q

                @pl.when(has_early)
                def _():
                    @pl.when(left_half)
                    def _():
                        outgoing[1] = wrap_out(q)

                    @pl.when(right_half)
                    def _():
                        outgoing[1] = q

                    late_copy().start()

            @pl.when(number == 4)
            def _():
                m = r_ref[...]
                y = y_ref[...]
                z = product(sig_ref[...], m)
                yt = product(y, t_ref[...])
                y_ref[...] = y + product(product(yt, z), uy_ref[...])
                q_ref[...] = product(m, q_ref[...])

        return carry

    lax.fori_loop(0, 5, stage, 0)

    def put(block, v):
        green_ref[0, block, 0] = v[:, :N]
        green_ref[0, block, 1] = v[:, N:]

    @pl.when(left_half)
    def _():
        put(0, q_ref[...])
        put(1, y_ref[...])

    @pl.when(right_half)
    def _():
        put(0, y_ref[...])
        put(1, q_ref[...])

    for number, o in enumerate(offsets):

        @pl.when(in_range(o))
        def _():
            occupancy_copy(number, o).wait_send()

    early_copy().wait_send()

    @pl.when(has_early)
    def _():
        late_copy().wait_send()


def local(
    lesser_occupancy,
    greater_occupancy,
    hamiltonian,
    couplings,
    right_lead,
    phonon_steps,
    emission_strength,
    absorption_strength,
):
    whole = pl.BlockSpec(memory_space=pltpu.VMEM)
    outside = pl.BlockSpec(memory_space=pltpu.HBM)
    mode_scalars = pltpu.SMEM((MODES,), jnp.float32)
    matrix = pltpu.VMEM((N, 2 * N), jnp.float32)
    pair = pltpu.VMEM((2, N, 2 * N), jnp.float32)
    reach = 2 * SMAX
    return pl.pallas_call(
        functools.partial(kernel, lax.axis_size("energy"), lax.axis_size("dom")),
        out_shape=(
            jax.ShapeDtypeStruct((1, 2, 2, N, N), jnp.float32),
            jax.ShapeDtypeStruct((1, 2, N), jnp.float32),
            jax.ShapeDtypeStruct((1, 2, N), jnp.float32),
        ),
        in_specs=[outside] * 8,
        out_specs=(whole,) * 3,
        scratch_shapes=[
            pltpu.SMEM((MODES,), jnp.int32),
            mode_scalars,
            mode_scalars,
            pltpu.VMEM(lesser_occupancy.shape, jnp.float32),
            pltpu.VMEM(greater_occupancy.shape, jnp.float32),
            pltpu.VMEM(hamiltonian.shape, jnp.float32),
            pltpu.VMEM(couplings.shape, jnp.float32),
            pltpu.VMEM(right_lead.shape, jnp.float32),
            pltpu.VMEM((8, N), jnp.float32),
            pltpu.VMEM((reach, 8, N), jnp.float32),
            pair,
            pair,
        ]
        + [matrix] * 20
        + [
            pltpu.SemaphoreType.DMA((reach,)),
            pltpu.SemaphoreType.DMA((reach,)),
            pltpu.SemaphoreType.DMA((2,)),
            pltpu.SemaphoreType.DMA((2,)),
            pltpu.SemaphoreType.DMA((8,)),
        ],
        compiler_params=pltpu.CompilerParams(
            collective_id=0, has_side_effects=True, vmem_limit_bytes=40 * 2**20
        ),
    )(
        phonon_steps,
        emission_strength,
        absorption_strength,
        lesser_occupancy,
        greater_occupancy,
        hamiltonian,
        couplings,
        right_lead,
    )


def solution(mesh):
    return jax.shard_map(
        local,
        mesh=mesh,
        in_specs=(
            P("energy", "dom", None),
            P("energy", "dom", None),
            P("dom", None, None, None),
            P("dom", None, None, None),
            P(),
            P(),
            P(),
            P(),
        ),
        out_specs=(
            P("energy", "dom", None, None, None),
            P("energy", "dom", None),
            P("energy", "dom", None),
        ),
        check_vma=False,
    )
```

```python
import functools

import jax
import jax.numpy as jnp
from jax import lax
from jax.experimental import pallas as pl
from jax.experimental.pallas import tpu as pltpu
from jax.sharding import PartitionSpec as P

MODES = 6
SMAX = 4
N = 128
H = 64
B = 8

energy_low = -1.0
energy_span = 2.0
damping = 0.02

MESH = pl.DeviceIdType.MESH


def parts(v):
    high = v.astype(jnp.bfloat16)
    return high, (v - high.astype(jnp.float32)).astype(jnp.bfloat16)


def real_product(a, b):
    a_high, a_low = parts(a)
    b_high, b_low = parts(b)
    dot = functools.partial(jnp.dot, preferred_element_type=jnp.float32)
    return dot(a_high, b_high) + (dot(a_high, b_low) + dot(a_low, b_high))


def product(a, b):
    h = b.shape[1] // 2
    turned_rows = jnp.concatenate([-b[:, h:], b[:, :h]], axis=1)
    return real_product(a, jnp.concatenate([b, turned_rows], axis=0))


def adjoint(a):
    return jnp.concatenate([a[:, :N].T, -a[:, N:].T], axis=1)


def identity():
    row = lax.broadcasted_iota(jnp.int32, (N, 2 * N), 0)
    lane = lax.broadcasted_iota(jnp.int32, (N, 2 * N), 1)
    return jnp.where(row == lane, 1.0, 0.0)


def times_i(a):
    r = pltpu.roll(a, H, axis=1)
    return jnp.where(lax.broadcasted_iota(jnp.int32, a.shape, 1) < H, -r, r)


def invert_half(x):
    shape = (B, N)
    row = lax.broadcasted_iota(jnp.int32, shape, 0)
    lane = lax.broadcasted_iota(jnp.int32, shape, 1)
    column = lane % H
    groups = [x[i * B : (i + 1) * B] for i in range(H // B)]
    count = len(groups)

    def along_lanes(v, c):
        return jnp.broadcast_to(v[:, c : c + 1], shape)

    def along_rows(v, k):
        return jnp.broadcast_to(v[k : k + 1], shape)

    zero = jnp.zeros(shape, jnp.float32)
    for p in range(count):
        panel = groups[p]
        turned = times_i(panel)
        br = [along_lanes(panel, p * B + j) for j in range(B)]
        bi = [along_lanes(panel, H + p * B + j) for j in range(B)]
        sr = zero
        si = zero
        for k in range(B):
            own = row == k
            mr = jnp.where(own, 0.0, br[k])
            mi = jnp.where(own, 0.0, bi[k])
            qr = along_rows(br[k], k)
            qi = along_rows(bi[k], k)
            s = 1.0 / (qr * qr + qi * qi)
            ur = (mr * qr + mi * qi) * s
            ui = (mi * qr - mr * qi) * s
            sr = jnp.where(own, qr * s, sr)
            si = jnp.where(own, -qi * s, si)
            for j in range(k + 1, B):
                yr = along_rows(br[j], k)
                yi = along_rows(bi[j], k)
                br[j] = br[j] - (ur * yr - ui * yi)
                bi[j] = bi[j] - (ur * yi + ui * yr)
            here = column == p * B + k
            panel = jnp.where(here, jnp.where(own & (lane < H), 1.0, 0.0), panel)
            turned = jnp.where(here, jnp.where(own & (lane >= H), 1.0, 0.0), turned)
            y = along_rows(panel, k)
            ty = along_rows(turned, k)
            panel = panel - (ur * y + ui * ty)
            turned = turned - (ur * ty - ui * y)
        panel, turned = sr * panel + si * turned, sr * turned - si * panel
        old = list(groups)
        groups[p] = panel
        inside = (column >= p * B) & (column < (p + 1) * B)
        spread = [zero] * p + [panel] + [zero] * (count - 1) + [turned] + [zero] * (count - 1 - p)
        change = real_product(jnp.concatenate(old, axis=0), jnp.concatenate(spread, axis=0))
        for g in range(count):
            if g == p:
                continue
            new = jnp.where(inside, 0.0, old[g])
            if g == p + 1:
                for j in range(B):
                    new = new - (
                        along_lanes(old[g], p * B + j) * along_rows(panel, j)
                        + along_lanes(old[g], H + p * B + j) * along_rows(turned, j)
                    )
            else:
                new = new - change[g * B : (g + 1) * B]
            groups[g] = new
    return jnp.concatenate(groups, axis=0)


def quarter(x, i, j):
    rows = x[i * H : (i + 1) * H]
    return jnp.concatenate(
        [rows[:, j * H : (j + 1) * H], rows[:, N + j * H : N + (j + 1) * H]], axis=1
    )


def invert_into(x, out_ref):
    a, b, c, d = quarter(x, 0, 0), quarter(x, 0, 1), quarter(x, 1, 0), quarter(x, 1, 1)
    e = invert_half(a)
    f = product(e, b)
    g = product(c, e)
    s = invert_half(d - product(c, f))
    fs = product(f, s)
    first = e + product(fs, g)
    across = -fs
    back = -product(s, g)
    out_ref[:H] = jnp.concatenate(
        [first[:, :H], across[:, :H], first[:, H:], across[:, H:]], axis=1
    )
    out_ref[H:] = jnp.concatenate([back[:, :H], s[:, :H], back[:, H:], s[:, H:]], axis=1)


def kernel(
    energy_count,
    partitions,
    steps_hbm,
    emission_hbm,
    absorption_hbm,
    lesser_hbm,
    greater_hbm,
    ham_hbm,
    coupling_hbm,
    lead_hbm,
    green_ref,
    in_ref,
    out_ref,
    steps_ref,
    emission_ref,
    absorption_ref,
    lesser_ref,
    greater_ref,
    ham_ref,
    coupling_ref,
    lead_ref,
    own_ref,
    window_ref,
    received,
    outgoing,
    a_first,
    a_second,
    c_fs,
    c_sf,
    w,
    wd,
    f_ref,
    u_ref,
    t_ref,
    s_ref,
    g_ref,
    th_ref,
    ht_ref,
    hb_ref,
    sig_ref,
    y_ref,
    uy_ref,
    q_ref,
    x_ref,
    r_ref,
    occ_send,
    occ_recv,
    dom_send,
    dom_recv,
    fetch_sems,
):
    fetches = [
        pltpu.make_async_copy(src, dst, fetch_sems.at[number])
        for number, (src, dst) in enumerate(
            (
                (lesser_hbm, lesser_ref),
                (greater_hbm, greater_ref),
                (coupling_hbm, coupling_ref),
                (lead_hbm, lead_ref),
                (steps_hbm, steps_ref),
                (emission_hbm, emission_ref),
                (absorption_hbm, absorption_ref),
                (ham_hbm, ham_ref),
            )
        )
    ]
    for fetch in fetches:
        fetch.start()
    energy = lax.axis_index("energy")
    dom = lax.axis_index("dom")
    half = (2 * dom >= partitions).astype(jnp.int32)
    left_half = half == 0
    right_half = half == 1
    has_early = jnp.where(left_half, dom, partitions - 1 - dom) > 0
    offsets = [o for o in range(-SMAX, SMAX + 1) if o != 0]

    def in_range(o):
        return (energy + o >= 0) & (energy + o < energy_count)

    barrier = pltpu.get_barrier_semaphore()
    greeted = jnp.int32(0)
    for o in offsets:
        there = in_range(o)
        greeted = greeted + there.astype(jnp.int32)

        @pl.when(there)
        def _():
            pl.semaphore_signal(
                barrier, inc=1, device_id={"energy": energy + o}, device_id_type=MESH
            )

    for o in (-1, 1):
        there = (dom + o >= 0) & (dom + o < partitions)
        greeted = greeted + there.astype(jnp.int32)

        @pl.when(there)
        def _():
            pl.semaphore_signal(barrier, inc=1, device_id={"dom": dom + o}, device_id_type=MESH)

    fetches[0].wait()
    fetches[1].wait()
    own_ref[0:2] = lesser_ref[0]
    own_ref[2:4] = greater_ref[0]
    own_ref[4:8] = jnp.zeros((4, N), jnp.float32)
    pl.semaphore_wait(barrier, greeted)

    def occupancy_copy(number, o):
        return pltpu.make_async_remote_copy(
            src_ref=own_ref,
            dst_ref=window_ref.at[len(offsets) - 1 - number],
            send_sem=occ_send.at[number],
            recv_sem=occ_recv.at[len(offsets) - 1 - number],
            device_id={"energy": energy + o},
            device_id_type=MESH,
        )

    for number, o in enumerate(offsets):
        there = in_range(o)

        @pl.when(there)
        def _():
            occupancy_copy(number, o).start()

        @pl.when(jnp.logical_not(there))
        def _():
            window_ref[number] = jnp.zeros((8, N), jnp.float32)

    for fetch in fetches[2:]:
        fetch.wait()
    link = jnp.concatenate([coupling_ref[1, 0], coupling_ref[1, 1]], axis=1)
    link_adjoint = adjoint(link)
    outer = jnp.concatenate([coupling_ref[0, 0], coupling_ref[0, 1]], axis=1)
    outer_adjoint = adjoint(outer)
    w[...] = outer
    wd[...] = outer_adjoint

    @pl.when(left_half)
    def _():
        c_fs[...] = link
        c_sf[...] = link_adjoint

    @pl.when(right_half)
    def _():
        c_fs[...] = link_adjoint
        c_sf[...] = link

    @pl.when(has_early)
    def _():
        x_ref[...] = jnp.zeros((N, 2 * N), jnp.float32)

    def half_i(a):
        return jnp.concatenate([-0.5 * a[:, N:], 0.5 * a[:, :N]], axis=1)

    @pl.when(dom == 0)
    def _():
        x_ref[...] = half_i(product(wd[...], w[...]))

    @pl.when(dom == partitions - 1)
    def _():
        lead = jnp.concatenate([lead_ref[0], lead_ref[1]], axis=1)
        x_ref[...] = half_i(product(lead, adjoint(lead)))

    for number, o in enumerate(offsets):

        @pl.when(in_range(o))
        def _():
            occupancy_copy(len(offsets) - 1 - number, -o).wait_recv()

    scattering_in = jnp.zeros((2, N), jnp.float32)
    scattering_out = jnp.zeros((2, N), jnp.float32)
    for step in range(1, SMAX + 1):
        emission = jnp.float32(0.0)
        absorption = jnp.float32(0.0)
        for m in range(MODES):
            chosen = steps_ref[m] == step
            emission = emission + jnp.where(chosen, emission_ref[m], 0.0)
            absorption = absorption + jnp.where(chosen, absorption_ref[m], 0.0)
        above = window_ref[offsets.index(step)]
        below = window_ref[offsets.index(-step)]
        scattering_in = scattering_in + emission * above[0:2] + absorption * below[0:2]
        scattering_out = scattering_out + emission * below[2:4] + absorption * above[2:4]
    in_ref[0] = scattering_in
    out_ref[0] = scattering_out
    broadening = 0.5 * (scattering_in + scattering_out)

    position = jnp.full((N, N), energy, jnp.int32).astype(jnp.float32)
    energy_value = energy_low + energy_span * (position + 0.5) / energy_count
    unit = identity()[:, :N]

    def system(b):
        real_part = unit * energy_value - ham_ref[b, 0]
        imag_part = unit * (damping + broadening[b : b + 1]) - ham_ref[b, 1]
        return jnp.concatenate([real_part, imag_part], axis=1)

    block_0 = system(0)
    block_1 = system(1)

    @pl.when(left_half)
    def _():
        a_first[...] = block_0 + x_ref[...]
        a_second[...] = block_1

    @pl.when(right_half)
    def _():
        a_first[...] = block_1 + x_ref[...]
        a_second[...] = block_0

    def early_copy():
        return pltpu.make_async_remote_copy(
            src_ref=outgoing.at[0],
            dst_ref=received.at[half],
            send_sem=dom_send.at[0],
            recv_sem=dom_recv.at[half],
            device_id={"dom": dom + 1 - 2 * half},
            device_id_type=MESH,
        )

    def late_copy():
        return pltpu.make_async_remote_copy(
            src_ref=outgoing.at[1],
            dst_ref=received.at[1 - half],
            send_sem=dom_send.at[1],
            recv_sem=dom_recv.at[1 - half],
            device_id={"dom": dom - 1 + 2 * half},
            device_id_type=MESH,
        )

    def wrap_out(v):
        return product(product(w[...], v), wd[...])

    def wrap_in(v):
        return product(product(wd[...], v), w[...])

    def send_early(v):
        @pl.when(left_half)
        def _():
            outgoing[0] = v

        @pl.when(right_half)
        def _():
            outgoing[0] = wrap_out(v)

        early_copy().start()

    def stage(number, carry):
        @pl.when(has_early | ((number != 2) & (number != 4)))
        def _():
            @pl.when(number == 0)
            def _():
                x_ref[...] = a_first[...]

            @pl.when(number == 1)
            def _():
                x_ref[...] = s_ref[...]

            @pl.when(number == 2)
            def _():
                early_copy().wait_recv()

                @pl.when(left_half)
                def _():
                    sig_ref[...] = wrap_in(received[0])

                @pl.when(right_half)
                def _():
                    sig_ref[...] = received[1]

                x_ref[...] = identity() - product(hb_ref[...], sig_ref[...])

            @pl.when(number == 3)
            def _():
                late_copy().wait_recv()

                @pl.when(left_half)
                def _():
                    x_ref[...] = s_ref[...] - received[1]

                @pl.when(right_half)
                def _():
                    x_ref[...] = s_ref[...] - wrap_in(received[0])

            @pl.when(number == 4)
            def _():
                x_ref[...] = identity() - product(q_ref[...], sig_ref[...])

            invert_into(x_ref[...], r_ref)

            @pl.when(number == 0)
            def _():
                f = r_ref[...]
                t = product(c_sf[...], f)
                f_ref[...] = f
                t_ref[...] = t
                s_ref[...] = a_second[...] - product(t, c_fs[...])
                u_ref[...] = product(f, c_fs[...])

            @pl.when(number == 1)
            def _():
                g = r_ref[...]
                g_ref[...] = g

                @pl.when(jnp.logical_not(has_early))
                def _():
                    send_early(g)

                @pl.when(has_early)
                def _():
                    ht = product(u_ref[...], g)
                    ht_ref[...] = ht
                    hb_ref[...] = f_ref[...] + product(ht, t_ref[...])
                    th_ref[...] = product(g, t_ref[...])

            @pl.when(number == 2)
            def _():
                z = product(sig_ref[...], r_ref[...])
                send_early(g_ref[...] + product(product(th_ref[...], z), ht_ref[...]))

            @pl.when(number == 3)
            def _():
                y = r_ref[...]
                uy = product(u_ref[...], y)
                q = f_ref[...] + product(uy, t_ref[...])
                y_ref[...] = y
                uy_ref[...] = uy
                q_ref[...] = q

                @pl.when(has_early)
                def _():
                    @pl.when(left_half)
                    def _():
                        outgoing[1] = wrap_out(q)

                    @pl.when(right_half)
                    def _():
                        outgoing[1] = q

                    late_copy().start()

            @pl.when(number == 4)
            def _():
                m = r_ref[...]
                y = y_ref[...]
                z = product(sig_ref[...], m)
                yt = product(y, t_ref[...])
                y_ref[...] = y + product(product(yt, z), uy_ref[...])
                q_ref[...] = product(m, q_ref[...])

        return carry

    lax.fori_loop(0, 5, stage, 0)

    def put(block, v):
        green_ref[0, block, 0] = v[:, :N]
        green_ref[0, block, 1] = v[:, N:]

    @pl.when(left_half)
    def _():
        put(0, q_ref[...])
        put(1, y_ref[...])

    @pl.when(right_half)
    def _():
        put(0, y_ref[...])
        put(1, q_ref[...])

    for number, o in enumerate(offsets):

        @pl.when(in_range(o))
        def _():
            occupancy_copy(number, o).wait_send()

    early_copy().wait_send()

    @pl.when(has_early)
    def _():
        late_copy().wait_send()


def local(
    lesser_occupancy,
    greater_occupancy,
    hamiltonian,
    couplings,
    right_lead,
    phonon_steps,
    emission_strength,
    absorption_strength,
):
    whole = pl.BlockSpec(memory_space=pltpu.VMEM)
    outside = pl.BlockSpec(memory_space=pltpu.HBM)
    mode_scalars = pltpu.SMEM((MODES,), jnp.float32)
    matrix = pltpu.VMEM((N, 2 * N), jnp.float32)
    pair = pltpu.VMEM((2, N, 2 * N), jnp.float32)
    reach = 2 * SMAX
    return pl.pallas_call(
        functools.partial(kernel, lax.axis_size("energy"), lax.axis_size("dom")),
        out_shape=(
            jax.ShapeDtypeStruct((1, 2, 2, N, N), jnp.float32),
            jax.ShapeDtypeStruct((1, 2, N), jnp.float32),
            jax.ShapeDtypeStruct((1, 2, N), jnp.float32),
        ),
        in_specs=[outside] * 8,
        out_specs=(whole,) * 3,
        scratch_shapes=[
            pltpu.SMEM((MODES,), jnp.int32),
            mode_scalars,
            mode_scalars,
            pltpu.VMEM(lesser_occupancy.shape, jnp.float32),
            pltpu.VMEM(greater_occupancy.shape, jnp.float32),
            pltpu.VMEM(hamiltonian.shape, jnp.float32),
            pltpu.VMEM(couplings.shape, jnp.float32),
            pltpu.VMEM(right_lead.shape, jnp.float32),
            pltpu.VMEM((8, N), jnp.float32),
            pltpu.VMEM((reach, 8, N), jnp.float32),
            pair,
            pair,
        ]
        + [matrix] * 20
        + [
            pltpu.SemaphoreType.DMA((reach,)),
            pltpu.SemaphoreType.DMA((reach,)),
            pltpu.SemaphoreType.DMA((2,)),
            pltpu.SemaphoreType.DMA((2,)),
            pltpu.SemaphoreType.DMA((8,)),
        ],
        compiler_params=pltpu.CompilerParams(
            collective_id=0, has_side_effects=True, vmem_limit_bytes=63 * 2**20 + 2**19
        ),
    )(
        phonon_steps,
        emission_strength,
        absorption_strength,
        lesser_occupancy,
        greater_occupancy,
        hamiltonian,
        couplings,
        right_lead,
    )


def solution(mesh):
    return jax.shard_map(
        local,
        mesh=mesh,
        in_specs=(
            P("energy", "dom", None),
            P("energy", "dom", None),
            P("dom", None, None, None),
            P("dom", None, None, None),
            P(),
            P(),
            P(),
            P(),
        ),
        out_specs=(
            P("energy", "dom", None, None, None),
            P("energy", "dom", None),
            P("energy", "dom", None),
        ),
        check_vma=False,
    )
```
